256 devices in a mesh: dp: 8 (over x, core), seq: 32 (over z, y).
Axes of the slice: x: 4, y: 4, z: 8, core: 2. Of those that a mesh axis runs over, the one named last changes fastest.
Arguments:
- query: bfloat16 [49152, 4096], P('seq', 'dp'), parts along dimension 1, may hold values from -6 to 6
- key_in: bfloat16 [49152, 4096], P('seq', 'dp'), parts along dimension 1, may hold values from -6 to 6
- value: bfloat16 [49152, 4096], P('seq', 'dp'), parts along dimension 1, may hold values from -6 to 6
- grad_out: bfloat16 [49152, 4096], P('seq', 'dp'), parts along dimension 1, may hold values from -6 to 6
Outputs:
- output: bfloat16 [49152, 4096], P('seq', 'dp'), parts along dimension 1
- grad_query: bfloat16 [49152, 4096], P('seq', 'dp'), parts along dimension 1
- grad_key: bfloat16 [49152, 4096], P('seq', 'dp'), parts along dimension 1
- grad_value: bfloat16 [49152, 4096], P('seq', 'dp'), parts along dimension 1
The draws below stay inside these ranges and needn't reach their ends.
There are 8 independent parts, one for each index of `dp`. The reference program is written for one: setup_inputs(seed, part) draws one part's arguments, and reference() takes and returns one part's arrays. A program takes and returns all parts, laid end to end along the dimension named above; each array names one. Nothing has to cross between parts.
All inputs are finite; a program needn't handle non-finite values.
Results may differ from the reference program's by a relative error of at most 0.0021.
Values sent between devices are 32-bit elements; how exact they have to be, the bound alone decides.
No kernel may reach another device: no remote copies, remote signals or barrier semaphores. Data moves between devices by JAX's collectives and lax.ppermute only.
A program may use at most 192 MiB of HBM per device.

```python
import math
import jax
import jax.numpy as jnp
from jax import lax

HEADS = 4
DH = 128
SPAN = 512
TOKENS = 49152


def block_scale(key, dims, shards, smallest, high):
    level = 1.0
    for dim, parts in shards:
        heights = jax.random.uniform(jax.random.fold_in(jax.random.fold_in(key, 6), dim), (parts,), jnp.float32, smallest / len(shards), high / len(shards))
        level = level * jnp.repeat(jnp.exp(heights), dims[dim] // parts).reshape((-1,) + (1,) * (len(dims) - 1 - dim))
    return level


def bell_draw(key, extent, scale, most, shards=(), kind=jnp.bfloat16):
    level = block_scale(key, extent, shards, -0.22, 0.18) if shards else 1.0
    result = jax.random.normal(key, extent, jnp.float32) * scale * level
    return jnp.minimum(jnp.maximum(result, -most), most).astype(kind)


def setup_inputs(seed: int = 0, part: int = 0) -> dict:
    keys = jax.random.split(jax.random.key(seed), 5)
    part_keys = jax.random.split(jax.random.fold_in(keys[4], part), 5)
    return {
        "query": bell_draw(part_keys[0], (TOKENS, HEADS * DH), 1.0, 6.0, ((0, 32),)),
        "key_in": bell_draw(part_keys[1], (TOKENS, HEADS * DH), 1.0, 6.0, ((0, 32),)),
        "value": bell_draw(part_keys[2], (TOKENS, HEADS * DH), 1.0, 6.0, ((0, 32),)),
        "grad_out": bell_draw(part_keys[3], (TOKENS, HEADS * DH), 1.0, 6.0, ((0, 32),)),
    }


def reference(query, key_in, value, grad_out):
    hp = lax.Precision.HIGHEST
    scale = 1.0 / math.sqrt(DH * TOKENS)
    blocks = TOKENS // SPAN

    def split(x):
        return x.reshape(blocks, SPAN, HEADS, DH).astype(jnp.float32)
    qf, kf, vf, gf = (split(query), split(key_in), split(value), split(grad_out))
    causal = (jnp.arange(SPAN)[:, None] >= jnp.arange(SPAN)[None, :]).astype(jnp.float32)
    kv_blocks = jnp.einsum('nshk,nshv->nhkv', kf, vf, precision=hp)
    qg_blocks = jnp.einsum('nthk,nthv->nhkv', qf, gf, precision=hp)
    zero = jnp.zeros((1, HEADS, DH, DH), jnp.float32)
    state_kv = jnp.concatenate([zero, jnp.cumsum(kv_blocks, axis=0)[:-1]], axis=0)
    state_qg = jnp.concatenate([jnp.cumsum(qg_blocks[::-1], axis=0)[:-1][::-1], zero], axis=0)
    scores = (scale * causal * jnp.einsum('nthk,nshk->nhts', qf, kf, precision=hp)).astype(jnp.bfloat16).astype(jnp.float32)
    gscores = (scale * causal * jnp.einsum('nthv,nshv->nhts', gf, vf, precision=hp)).astype(jnp.bfloat16).astype(jnp.float32)
    output = jnp.einsum('nhts,nshv->nthv', scores, vf, precision=hp) + scale * jnp.einsum('nthk,nhkv->nthv', qf, state_kv, precision=hp)
    grad_query = jnp.einsum('nhts,nshk->nthk', gscores, kf, precision=hp) + scale * jnp.einsum('nthv,nhkv->nthk', gf, state_kv, precision=hp)
    grad_key = jnp.einsum('nhts,nthk->nshk', gscores, qf, precision=hp) + scale * jnp.einsum('nshv,nhkv->nshk', vf, state_qg, precision=hp)
    grad_value = jnp.einsum('nhts,nthv->nshv', scores, gf, precision=hp) + scale * jnp.einsum('nshk,nhkv->nshv', kf, state_qg, precision=hp)

    def back(x):
        return x.reshape(TOKENS, HEADS * DH).astype(jnp.bfloat16)
    return (back(output), back(grad_query), back(grad_key), back(grad_value))
```

```python
import functools
import math

import jax
import jax.numpy as jnp
from jax import lax
from jax.experimental import pallas as pl
from jax.experimental.pallas import tpu as pltpu
from jax.sharding import PartitionSpec as P

DH = 128
SPAN = 512
HALF = SPAN // 2
HEADS = 4
NY = 4
NZ = 8
LOCAL_FLOPS = 2_000_000_000
F32 = jnp.float32
BF16 = jnp.bfloat16
VM = pl.BlockSpec(memory_space=pltpu.VMEM)
SM = pl.BlockSpec(memory_space=pltpu.SMEM)
HB = pl.BlockSpec(memory_space=pltpu.HBM)


def dot(a, b, ca, cb):
    return lax.dot_general(a, b, (((ca,), (cb,)), ((), ())), preferred_element_type=F32)


def twice(x):
    return jnp.concatenate([x, x], axis=1)


def stacked(s, axis):
    hi = s.astype(BF16)
    lo = (s - hi.astype(F32)).astype(BF16)
    return jnp.concatenate([hi, lo], axis=axis)


def at(n, h):
    return slice(n * SPAN, (n + 1) * SPAN), slice(h * DH, (h + 1) * DH)


CHUNKS = ((0, 512), (512, 512), (1024, 256), (1280, 256))


def head_sums(me_ref, xs, d, out, cum):
    q, k, v, g = xs
    cols = pl.ds(pl.multiple_of(((me_ref[0] + d) & 3) * DH, DH), DH)
    state = {"kv": 0.0, "first": 0.0}

    def step(n):
        start, size = CHUNKS[n]
        block, r = start // SPAN, slice(start, start + size)
        qg = dot(q[r, cols], g[r, cols], 0, 0)
        state["kv"] = state["kv"] + dot(k[r, cols], v[r, cols], 0, 0)
        for j in range(min(block, cum.shape[0])):
            if block == j + 1 and start % SPAN == 0:
                cum[j, DH:] = qg
            else:
                cum[j, DH:] += qg
        if block == 0:
            state["first"] = state["first"] + qg
        if (start + size) % SPAN == 0 and block < cum.shape[0]:
            cum[block, :DH] = state["kv"]

    def finish():
        out[:DH] = state["kv"]
        out[DH:] = state["first"] + cum[0, DH:]

    return step, finish


def sums_kernel(me_ref, high_ref, up_ref, *refs):
    srcs, dsts, outs, cum, sems = refs[:4], refs[4:8], refs[8:11], refs[11], refs[12]
    copies = []
    for n, (start, size) in enumerate(CHUNKS):
        rows = pl.ds(start, size)
        copies.append([pltpu.make_async_copy(srcs[i].at[rows], dsts[i].at[rows], sems.at[n, i]) for i in range(4)])
    for row in copies:
        for c in row:
            c.start()
    heads = [head_sums(me_ref, dsts, d + 1, outs[d], cum.at[d]) for d in range(3)]
    for n in range(len(CHUNKS)):
        for c in copies[n]:
            c.wait()
        for step, _ in heads:
            step(n)
    for _, finish in heads:
        finish()


def device_sums(me, high, up, q, k, v, g):
    rows, width = q.shape
    one = jax.ShapeDtypeStruct((2 * DH, DH), F32)
    return pl.pallas_call(
        sums_kernel,
        in_specs=[SM] * 3 + [HB] * 4,
        out_specs=[VM] * 8,
        out_shape=[pltpu.VMEM((rows, width), BF16)] * 4 + [one] * 3 + [pltpu.VMEM((3, rows // SPAN - 1, 2 * DH, DH), F32)],
        scratch_shapes=[pltpu.SemaphoreType.DMA((len(CHUNKS), 4))],
        compiler_params=pltpu.CompilerParams(vmem_limit_bytes=16 * 2**20),
        name="device_sums",
    )(me, high, up, q, k, v, g)


def own_kernel(me_ref, q, k, v, g, out, cum):
    step, finish = head_sums(me_ref, (q, k, v, g), 0, out, cum.at[0])
    for n in range(len(CHUNKS)):
        step(n)
    finish()


def own_sums(me, xs):
    rows = xs[0].shape[0]
    return pl.pallas_call(
        own_kernel,
        in_specs=[SM] + [VM] * 4,
        out_specs=[VM] * 2,
        out_shape=[jax.ShapeDtypeStruct((2 * DH, DH), F32), pltpu.VMEM((1, rows // SPAN - 1, 2 * DH, DH), F32)],
        compiler_params=pltpu.CompilerParams(vmem_limit_bytes=8 * 2**20),
        cost_estimate=pl.CostEstimate(flops=100_000_000, bytes_accessed=1024, transcendentals=0),
        name="own_sums",
    )(me, *xs)


def local_kernel(scale, h, blocks, q_ref, k_ref, v_ref, g_ref, *refs):
    o_ref, gq_ref, gk_ref, gv_ref = refs[-4:]
    cols = slice(h * DH, (h + 1) * DH)
    t = lax.broadcasted_iota(jnp.int32, (HALF, HALF), 0)
    s = lax.broadcasted_iota(jnp.int32, (HALF, HALF), 1)
    keep = t >= s

    def lower(a, b):
        top = jnp.where(keep, scale * dot(a[:HALF], b[:HALF], 1, 1), 0.0).astype(BF16)
        low = scale * dot(a[HALF:], b, 1, 1)
        right = jnp.where(keep, low[:, HALF:], 0.0)
        return top, jnp.concatenate([low[:, :HALF].astype(BF16), right.astype(BF16)], axis=1)

    def across(top, low, x):
        return jnp.concatenate([dot(top, x[:HALF], 1, 0), dot(low, x, 1, 0)], axis=0)

    def down(top, low, x):
        both = dot(low, x[HALF:], 0, 0)
        return jnp.concatenate([dot(top, x[:HALF], 0, 0) + both[:HALF], both[HALF:]], axis=0)

    for n in range(blocks):
        r = slice(n * SPAN, (n + 1) * SPAN)
        q, k, v, g = q_ref[r, cols], k_ref[r, cols], v_ref[r, cols], g_ref[r, cols]
        s0, s1 = lower(q, k)
        d0, d1 = lower(g, v)
        o_ref[r, cols] = across(s0, s1, v)
        gq_ref[r, cols] = across(d0, d1, k)
        gk_ref[r, cols] = down(d0, d1, q)
        gv_ref[r, cols] = down(s0, s1, g)


def local_products(scale, h, xs, parts):
    rows, width = xs[0].shape
    blocks = rows // SPAN
    return pl.pallas_call(
        functools.partial(local_kernel, scale, h, blocks),
        in_specs=[VM] * (4 + len(parts)),
        out_specs=[VM] * 4,
        out_shape=[pltpu.VMEM((rows, width), F32)] * 4,
        input_output_aliases={4 + i: i for i in range(len(parts))},
        compiler_params=pltpu.CompilerParams(vmem_limit_bytes=16 * 2**20),
        cost_estimate=pl.CostEstimate(flops=LOCAL_FLOPS, bytes_accessed=1024, transcendentals=0),
        name="local_products",
    )(*xs, *parts)


def ready_kernel(me_ref, g0, g1, g2, g3, pair, *outs):
    y, z = me_ref[0] & 3, me_ref[0] >> 2
    got = [(r[:DH], r[DH:]) for r in (g0, g1, g2, g3)]

    def when(c, x):
        return jnp.where(c, x, 0.0)

    kv = when((z & 1) != 0, pair[:DH])
    qg = when((z & 1) == 0, pair[DH:])
    for e, out in enumerate(outs):
        dst = (y + e) & 3
        a, b = kv, qg
        for d in range(NY):
            src = (y - d) & 3
            a = a + when(src < dst, got[d][0])
            b = b + when(src > dst, got[d][1])
        out[:DH] = a
        out[DH:] = b


def make_ready(me, *arrays):
    return pl.pallas_call(
        ready_kernel,
        in_specs=[SM] + [VM] * len(arrays),
        out_specs=[VM] * NY,
        out_shape=[jax.ShapeDtypeStruct((2 * DH, DH), F32)] * NY,
        compiler_params=pltpu.CompilerParams(vmem_limit_bytes=8 * 2**20),
        name="make_ready",
    )(me, *arrays)


def carry_kernel(scale, steps, blocks, me_ref, *refs):
    xs, parts, cums, refs = refs[:4], refs[4:8], refs[8:10], refs[10:]
    priors, outs, stage, sems = refs[: len(steps)], refs[-6:-2], refs[-2], refs[-1]
    q, k, v, g = xs
    copies = []
    for i, (d, prior) in enumerate(zip(steps, priors)):
        h = (me_ref[0] - d) & 3
        cols = pl.ds(pl.multiple_of(h * DH, DH), DH)
        cum = cums[1].at[HEADS - 1 - d] if d else cums[0].at[0]
        for n in range(blocks):
            kv, qg = prior[:DH], prior[DH:]
            if n > 0:
                kv = kv + cum[n - 1, :DH]
            if n < blocks - 1:
                qg = qg + cum[n, DH:]
            kv, qg = kv * scale, qg * scale
            r = pl.ds(n * SPAN, SPAN)
            todo = ((q, stacked(kv, 0), 0), (g, stacked(kv, 1), 1), (v, stacked(qg, 1), 1), (k, stacked(qg, 0), 0))
            for j, (x, w, c) in enumerate(todo):
                add = dot(twice(x[r, cols]), w, 1, c)
                stage[i, j, r] = (parts[j][r, cols] + add).astype(BF16)
                copy = pltpu.make_async_copy(stage.at[i, j, r], outs[j].at[r, cols], sems.at[i, j, n])
                copy.start()
                copies.append(copy)
    for copy in copies:
        copy.wait()


def add_carry(scale, me, steps, xs, parts, cums, priors, before):
    rows, width = xs[0].shape
    blocks = rows // SPAN
    m = len(steps)
    return pl.pallas_call(
        functools.partial(carry_kernel, scale, steps, blocks),
        in_specs=[SM] + [VM] * (10 + m) + [HB] * len(before),
        out_specs=[HB] * 4,
        out_shape=[pltpu.HBM((rows, width), BF16)] * 4,
        input_output_aliases={11 + m + i: i for i in range(len(before))},
        scratch_shapes=[pltpu.VMEM((m, 4, rows, DH), BF16), pltpu.SemaphoreType.DMA((m, 4, blocks))],
        compiler_params=pltpu.CompilerParams(vmem_limit_bytes=16 * 2**20),
        cost_estimate=pl.CostEstimate(flops=m * 1_500_000_000, bytes_accessed=1024, transcendentals=0),
        name="add_carry",
    )(me, *xs, *parts, *cums, *priors, *before)


def moves(zmap, ymap):
    return [(z * NY + y, zmap(z) * NY + ymap(y)) for z in range(NZ) for y in range(NY)]


def on_device(query, key_in, value, grad_out):
    rows = query.shape[0]
    scale = 1.0 / math.sqrt(DH * rows * lax.axis_size("seq"))
    blocks = rows // SPAN
    index = lax.axis_index("seq")
    me = index.reshape(1)
    inputs = [pltpu.with_memory_space_constraint(x, pltpu.HBM) for x in (query, key_in, value, grad_out)]

    def swap(x, zmap):
        return lax.ppermute(x, "seq", moves(zmap, lambda b: b))

    def turn(x, d):
        return lax.ppermute(x, "seq", moves(lambda a: a, lambda b: (b + d) % NY))

    high, up = index >= NY * NZ // 2, (index & (2 * NY)) != 0
    flags = [c.astype(jnp.int32).reshape(1) for c in (high, up)]
    q, k, v, g, *own, others = device_sums(me, *flags, *inputs)
    xs = (q, k, v, g)
    sent = [turn(own[d - 1], d) for d in range(1, NY)]
    mine, inner = own_sums(me, xs)
    got = [mine] + sent
    parts = ()
    for h in range(HEADS):
        parts = local_products(scale, h, xs, parts)
    total = got[0] + got[1] + got[2] + got[3]
    pair = swap(total, lambda a: a ^ 1)
    total = total + pair
    four = swap(jnp.where(up, total[DH:], total[:DH]), lambda a: a ^ 3)
    across = jnp.where(high, total[DH:], total[:DH])
    eight = swap(across, lambda a: a ^ 5), swap(across, lambda a: 7 - a)
    eight = eight[0] + eight[1]
    last = jnp.concatenate(
        [
            jnp.where(up, four, 0.0) + jnp.where(high, eight, 0.0),
            jnp.where(up, 0.0, four) + jnp.where(high, 0.0, eight),
        ],
        axis=0,
    )
    ready = [x + last for x in make_ready(me, *got, pair)]
    prior = {0: ready[0]} | {d: turn(ready[d], d) for d in (2, 3, 1)}
    outs = ()
    for steps in ((0,), (3,), (2, 1)):
        outs = add_carry(scale, me, steps, xs, parts, (inner, others), [prior[d] for d in steps], outs)
    return tuple(outs)


def solution(mesh):
    spec = P("seq", "dp")
    return jax.shard_map(
        on_device,
        mesh=mesh,
        in_specs=(spec,) * 4,
        out_specs=(spec,) * 4,
        check_vma=False,
    )
```

```python
import functools
import math

import jax
import jax.numpy as jnp
from jax import lax
from jax.experimental import pallas as pl
from jax.experimental.pallas import tpu as pltpu
from jax.sharding import PartitionSpec as P

DH = 128
SPAN = 512
HALF = SPAN // 2
HEADS = 4
NY = 4
NZ = 8
LOCAL_FLOPS = 2_000_000_000
F32 = jnp.float32
BF16 = jnp.bfloat16
VM = pl.BlockSpec(memory_space=pltpu.VMEM)
SM = pl.BlockSpec(memory_space=pltpu.SMEM)
HB = pl.BlockSpec(memory_space=pltpu.HBM)


def dot(a, b, ca, cb):
    return lax.dot_general(a, b, (((ca,), (cb,)), ((), ())), preferred_element_type=F32)


def twice(x):
    return jnp.concatenate([x, x], axis=1)


def stacked(s, axis):
    hi = s.astype(BF16)
    lo = (s - hi.astype(F32)).astype(BF16)
    return jnp.concatenate([hi, lo], axis=axis)


def at(n, h):
    return slice(n * SPAN, (n + 1) * SPAN), slice(h * DH, (h + 1) * DH)


CHUNKS = ((0, 512), (512, 512), (1024, 256), (1280, 256))


def head_sums(me_ref, xs, d, out, cum):
    q, k, v, g = xs
    cols = pl.ds(pl.multiple_of(((me_ref[0] + d) & 3) * DH, DH), DH)
    state = {"kv": 0.0, "first": 0.0}

    def step(n):
        start, size = CHUNKS[n]
        block, r = start // SPAN, slice(start, start + size)
        qg = dot(q[r, cols], g[r, cols], 0, 0)
        state["kv"] = state["kv"] + dot(k[r, cols], v[r, cols], 0, 0)
        for j in range(min(block, cum.shape[0])):
            if block == j + 1 and start % SPAN == 0:
                cum[j, DH:] = qg
            else:
                cum[j, DH:] += qg
        if block == 0:
            state["first"] = state["first"] + qg
        if (start + size) % SPAN == 0 and block < cum.shape[0]:
            cum[block, :DH] = state["kv"]

    def finish():
        out[:DH] = state["kv"]
        out[DH:] = state["first"] + cum[0, DH:]

    return step, finish


def sums_kernel(me_ref, high_ref, up_ref, *refs):
    srcs, dsts, outs, cum, sems = refs[:4], refs[4:8], refs[8:11], refs[11], refs[12]
    copies = []
    for n, (start, size) in enumerate(CHUNKS):
        rows = pl.ds(start, size)
        copies.append([pltpu.make_async_copy(srcs[i].at[rows], dsts[i].at[rows], sems.at[n, i]) for i in range(4)])
    for row in copies:
        for c in row:
            c.start()
    heads = [head_sums(me_ref, dsts, d + 1, outs[d], cum.at[d]) for d in range(3)]
    for n in range(len(CHUNKS)):
        for c in copies[n]:
            c.wait()
        for step, _ in heads:
            step(n)
    for _, finish in heads:
        finish()


def device_sums(me, high, up, q, k, v, g):
    rows, width = q.shape
    one = jax.ShapeDtypeStruct((2 * DH, DH), F32)
    return pl.pallas_call(
        sums_kernel,
        in_specs=[SM] * 3 + [HB] * 4,
        out_specs=[VM] * 8,
        out_shape=[pltpu.VMEM((rows, width), BF16)] * 4 + [one] * 3 + [pltpu.VMEM((3, rows // SPAN - 1, 2 * DH, DH), F32)],
        scratch_shapes=[pltpu.SemaphoreType.DMA((len(CHUNKS), 4))],
        compiler_params=pltpu.CompilerParams(vmem_limit_bytes=16 * 2**20),
        name="device_sums",
    )(me, high, up, q, k, v, g)


def own_kernel(me_ref, q, k, v, g, out, cum):
    step, finish = head_sums(me_ref, (q, k, v, g), 0, out, cum.at[0])
    for n in range(len(CHUNKS)):
        step(n)
    finish()


def own_sums(me, xs):
    rows = xs[0].shape[0]
    return pl.pallas_call(
        own_kernel,
        in_specs=[SM] + [VM] * 4,
        out_specs=[VM] * 2,
        out_shape=[jax.ShapeDtypeStruct((2 * DH, DH), F32), pltpu.VMEM((1, rows // SPAN - 1, 2 * DH, DH), F32)],
        compiler_params=pltpu.CompilerParams(vmem_limit_bytes=8 * 2**20),
        cost_estimate=pl.CostEstimate(flops=100_000_000, bytes_accessed=1024, transcendentals=0),
        name="own_sums",
    )(me, *xs)


def local_kernel(scale, h, blocks, q_ref, k_ref, v_ref, g_ref, *refs):
    o_ref, gq_ref, gk_ref, gv_ref = refs[-4:]
    cols = slice(h * DH, (h + 1) * DH)
    t = lax.broadcasted_iota(jnp.int32, (HALF, HALF), 0)
    s = lax.broadcasted_iota(jnp.int32, (HALF, HALF), 1)
    keep = t >= s

    def lower(a, b):
        top = jnp.where(keep, scale * dot(a[:HALF], b[:HALF], 1, 1), 0.0).astype(BF16)
        low = scale * dot(a[HALF:], b, 1, 1)
        right = jnp.where(keep, low[:, HALF:], 0.0)
        return top, jnp.concatenate([low[:, :HALF].astype(BF16), right.astype(BF16)], axis=1)

    def across(top, low, x):
        return jnp.concatenate([dot(top, x[:HALF], 1, 0), dot(low, x, 1, 0)], axis=0)

    def down(top, low, x):
        both = dot(low, x[HALF:], 0, 0)
        return jnp.concatenate([dot(top, x[:HALF], 0, 0) + both[:HALF], both[HALF:]], axis=0)

    for n in range(blocks):
        r = slice(n * SPAN, (n + 1) * SPAN)
        q, k, v, g = q_ref[r, cols], k_ref[r, cols], v_ref[r, cols], g_ref[r, cols]
        s0, s1 = lower(q, k)
        d0, d1 = lower(g, v)
        o_ref[r, cols] = across(s0, s1, v)
        gq_ref[r, cols] = across(d0, d1, k)
        gk_ref[r, cols] = down(d0, d1, q)
        gv_ref[r, cols] = down(s0, s1, g)


def local_products(scale, h, xs, parts):
    rows, width = xs[0].shape
    blocks = rows // SPAN
    return pl.pallas_call(
        functools.partial(local_kernel, scale, h, blocks),
        in_specs=[VM] * (4 + len(parts)),
        out_specs=[VM] * 4,
        out_shape=[pltpu.VMEM((rows, width), F32)] * 4,
        input_output_aliases={4 + i: i for i in range(len(parts))},
        compiler_params=pltpu.CompilerParams(vmem_limit_bytes=16 * 2**20),
        cost_estimate=pl.CostEstimate(flops=LOCAL_FLOPS, bytes_accessed=1024, transcendentals=0),
        name="local_products",
    )(*xs, *parts)


def ready_kernel(me_ref, g0, g1, g2, g3, pair, *outs):
    y, z = me_ref[0] & 3, me_ref[0] >> 2
    got = [(r[:DH], r[DH:]) for r in (g0, g1, g2, g3)]

    def when(c, x):
        return jnp.where(c, x, 0.0)

    kv = when((z & 1) != 0, pair[:DH])
    qg = when((z & 1) == 0, pair[DH:])
    for e, out in enumerate(outs):
        dst = (y + e) & 3
        a, b = kv, qg
        for d in range(NY):
            src = (y - d) & 3
            a = a + when(src < dst, got[d][0])
            b = b + when(src > dst, got[d][1])
        out[:DH] = a
        out[DH:] = b


def make_ready(me, *arrays):
    return pl.pallas_call(
        ready_kernel,
        in_specs=[SM] + [VM] * len(arrays),
        out_specs=[VM] * NY,
        out_shape=[jax.ShapeDtypeStruct((2 * DH, DH), F32)] * NY,
        compiler_params=pltpu.CompilerParams(vmem_limit_bytes=8 * 2**20),
        name="make_ready",
    )(me, *arrays)


def carry_kernel(scale, steps, blocks, me_ref, *refs):
    xs, parts, cums, refs = refs[:4], refs[4:8], refs[8:10], refs[10:]
    priors, outs, stage, sems = refs[: len(steps)], refs[-6:-2], refs[-2], refs[-1]
    q, k, v, g = xs
    copies = []
    for i, (d, prior) in enumerate(zip(steps, priors)):
        h = (me_ref[0] - d) & 3
        cols = pl.ds(pl.multiple_of(h * DH, DH), DH)
        cum = cums[1].at[HEADS - 1 - d] if d else cums[0].at[0]
        for n in range(blocks):
            kv, qg = prior[:DH], prior[DH:]
            if n > 0:
                kv = kv + cum[n - 1, :DH]
            if n < blocks - 1:
                qg = qg + cum[n, DH:]
            kv, qg = kv * scale, qg * scale
            todo = ((q, stacked(kv, 0), 0), (g, stacked(kv, 1), 1), (v, stacked(qg, 1), 1), (k, stacked(qg, 0), 0))
            end = n == blocks - 1 and i == len(steps) - 1
            for m, part in enumerate((HALF, HALF) if end else (SPAN,)):
                r = pl.ds(n * SPAN + m * HALF, part)
                for j, (x, w, c) in enumerate(todo):
                    add = dot(twice(x[r, cols]), w, 1, c)
                    stage[i, j, r] = (parts[j][r, cols] + add).astype(BF16)
                    copy = pltpu.make_async_copy(stage.at[i, j, r], outs[j].at[r, cols], sems.at[i, j, n + m])
                    copy.start()
                    copies.append(copy)
    for copy in copies:
        copy.wait()


def add_carry(scale, me, steps, xs, parts, cums, priors, before):
    rows, width = xs[0].shape
    blocks = rows // SPAN
    m = len(steps)
    return pl.pallas_call(
        functools.partial(carry_kernel, scale, steps, blocks),
        in_specs=[SM] + [VM] * (10 + m) + [HB] * len(before),
        out_specs=[HB] * 4,
        out_shape=[pltpu.HBM((rows, width), BF16)] * 4,
        input_output_aliases={11 + m + i: i for i in range(len(before))},
        scratch_shapes=[pltpu.VMEM((m, 4, rows, DH), BF16), pltpu.SemaphoreType.DMA((m, 4, blocks + 1))],
        compiler_params=pltpu.CompilerParams(vmem_limit_bytes=16 * 2**20),
        cost_estimate=pl.CostEstimate(flops=m * 1_500_000_000, bytes_accessed=1024, transcendentals=0),
        name="add_carry",
    )(me, *xs, *parts, *cums, *priors, *before)


def moves(zmap, ymap):
    return [(z * NY + y, zmap(z) * NY + ymap(y)) for z in range(NZ) for y in range(NY)]


def on_device(query, key_in, value, grad_out):
    rows = query.shape[0]
    scale = 1.0 / math.sqrt(DH * rows * lax.axis_size("seq"))
    blocks = rows // SPAN
    index = lax.axis_index("seq")
    me = index.reshape(1)
    inputs = [pltpu.with_memory_space_constraint(x, pltpu.HBM) for x in (query, key_in, value, grad_out)]

    def swap(x, zmap):
        return lax.ppermute(x, "seq", moves(zmap, lambda b: b))

    def turn(x, d):
        return lax.ppermute(x, "seq", moves(lambda a: a, lambda b: (b + d) % NY))

    high, up = index >= NY * NZ // 2, (index & (2 * NY)) != 0
    flags = [c.astype(jnp.int32).reshape(1) for c in (high, up)]
    q, k, v, g, *own, others = device_sums(me, *flags, *inputs)
    xs = (q, k, v, g)
    sent = [turn(own[d - 1], d) for d in range(1, NY)]
    mine, inner = own_sums(me, xs)
    got = [mine] + sent
    parts = ()
    for h in range(HEADS):
        parts = local_products(scale, h, xs, parts)
    total = got[0] + got[1] + got[2] + got[3]
    pair = swap(total, lambda a: a ^ 1)
    total = total + pair
    four = swap(jnp.where(up, total[DH:], total[:DH]), lambda a: a ^ 3)
    across = jnp.where(high, total[DH:], total[:DH])
    eight = swap(across, lambda a: a ^ 5), swap(across, lambda a: 7 - a)
    eight = eight[0] + eight[1]
    last = jnp.concatenate(
        [
            jnp.where(up, four, 0.0) + jnp.where(high, eight, 0.0),
            jnp.where(up, 0.0, four) + jnp.where(high, 0.0, eight),
        ],
        axis=0,
    )
    ready = [x + last for x in make_ready(me, *got, pair)]
    prior = {0: ready[0]} | {d: turn(ready[d], d) for d in (2, 3, 1)}
    outs = ()
    for steps in ((0,), (1, 2, 3)):
        outs = add_carry(scale, me, steps, xs, parts, (inner, others), [prior[d] for d in steps], outs)
    return tuple(outs)


def solution(mesh):
    spec = P("seq", "dp")
    return jax.shard_map(
        on_device,
        mesh=mesh,
        in_specs=(spec,) * 4,
        out_specs=(spec,) * 4,
        check_vma=False,
    )
```

```python
import functools
import math

import jax
import jax.numpy as jnp
from jax import lax
from jax.experimental import pallas as pl
from jax.experimental.pallas import tpu as pltpu
from jax.sharding import PartitionSpec as P

DH = 128
SPAN = 512
HALF = SPAN // 2
HEADS = 4
NY = 4
NZ = 8
LOCAL_FLOPS = 2_000_000_000
F32 = jnp.float32
BF16 = jnp.bfloat16
VM = pl.BlockSpec(memory_space=pltpu.VMEM)
HB = pl.BlockSpec(memory_space=pltpu.HBM)


def side():
    return 1 - 2 * (lax.axis_index("dp") & 1)


def dot(a, b, ca, cb):
    return lax.dot_general(a, b, (((ca,), (cb,)), ((), ())), preferred_element_type=F32)


def twice(x):
    return jnp.concatenate([x, x], axis=1)


def stacked(s, axis):
    hi = s.astype(BF16)
    lo = (s - hi.astype(F32)).astype(BF16)
    return jnp.concatenate([hi, lo], axis=axis)


def at(n, h):
    return slice(n * SPAN, (n + 1) * SPAN), slice(h * DH, (h + 1) * DH)


CHUNKS = ((0, 512), (512, 512), (1024, 256), (1280, 256))


def head_sums(xs, d, out, cum):
    q, k, v, g = xs
    cols = pl.ds(pl.multiple_of(((lax.axis_index("seq") + side() * d) & 3) * DH, DH), DH)
    state = {"kv": 0.0, "first": 0.0}

    def step(n):
        start, size = CHUNKS[n]
        block, r = start // SPAN, slice(start, start + size)
        qg = dot(q[r, cols], g[r, cols], 0, 0)
        state["kv"] = state["kv"] + dot(k[r, cols], v[r, cols], 0, 0)
        for j in range(min(block, cum.shape[0])):
            if block == j + 1 and start % SPAN == 0:
                cum[j, DH:] = qg
            else:
                cum[j, DH:] += qg
        if block == 0:
            state["first"] = state["first"] + qg
        if (start + size) % SPAN == 0 and block < cum.shape[0]:
            cum[block, :DH] = state["kv"]

    def finish():
        out[:DH] = state["kv"]
        out[DH:] = state["first"] + cum[0, DH:]

    return step, finish


def sums_kernel(*refs):
    srcs, dsts, outs, cum, high, up, sems = refs[:4], refs[4:8], refs[8:11], refs[11], refs[12], refs[13], refs[14]
    copies = []
    for n, (start, size) in enumerate(CHUNKS):
        rows = pl.ds(start, size)
        copies.append([pltpu.make_async_copy(srcs[i].at[rows], dsts[i].at[rows], sems.at[n, i]) for i in range(4)])
    for row in copies:
        for c in row:
            c.start()
    z = lax.axis_index("seq") >> 2
    high[...] = jnp.full(high.shape, z >> 2, jnp.int32).astype(F32)
    up[...] = jnp.full(up.shape, (z >> 1) & 1, jnp.int32).astype(F32)
    heads = [head_sums(dsts, d + 1, outs[d], cum.at[d]) for d in range(3)]
    for n in range(len(CHUNKS)):
        for c in copies[n]:
            c.wait()
        for step, _ in heads:
            step(n)
    for _, finish in heads:
        finish()


def device_sums(q, k, v, g):
    rows, width = q.shape
    one = jax.ShapeDtypeStruct((2 * DH, DH), F32)
    return pl.pallas_call(
        sums_kernel,
        in_specs=[HB] * 4,
        out_specs=[VM] * 10,
        out_shape=[pltpu.VMEM((rows, width), BF16)] * 4 + [one] * 3 + [pltpu.VMEM((3, rows // SPAN - 1, 2 * DH, DH), F32)]
        + [jax.ShapeDtypeStruct((DH, DH), F32)] * 2,
        scratch_shapes=[pltpu.SemaphoreType.DMA((len(CHUNKS), 4))],
        compiler_params=pltpu.CompilerParams(vmem_limit_bytes=16 * 2**20),
        name="device_sums",
    )(q, k, v, g)


def own_kernel(q, k, v, g, out, cum):
    step, finish = head_sums((q, k, v, g), 0, out, cum.at[0])
    for n in range(len(CHUNKS)):
        step(n)
    finish()


def own_sums(xs):
    rows = xs[0].shape[0]
    return pl.pallas_call(
        own_kernel,
        in_specs=[VM] * 4,
        out_specs=[VM] * 2,
        out_shape=[jax.ShapeDtypeStruct((2 * DH, DH), F32), pltpu.VMEM((1, rows // SPAN - 1, 2 * DH, DH), F32)],
        compiler_params=pltpu.CompilerParams(vmem_limit_bytes=8 * 2**20),
        cost_estimate=pl.CostEstimate(flops=100_000_000, bytes_accessed=1024, transcendentals=0),
        name="own_sums",
    )(*xs)


def local_kernel(scale, h, blocks, q_ref, k_ref, v_ref, g_ref, *refs):
    o_ref, gq_ref, gk_ref, gv_ref = refs[-4:]
    cols = slice(h * DH, (h + 1) * DH)
    t = lax.broadcasted_iota(jnp.int32, (HALF, HALF), 0)
    s = lax.broadcasted_iota(jnp.int32, (HALF, HALF), 1)
    keep = t >= s

    def lower(a, b):
        top = jnp.where(keep, scale * dot(a[:HALF], b[:HALF], 1, 1), 0.0).astype(BF16)
        low = scale * dot(a[HALF:], b, 1, 1)
        right = jnp.where(keep, low[:, HALF:], 0.0)
        return top, jnp.concatenate([low[:, :HALF].astype(BF16), right.astype(BF16)], axis=1)

    def across(top, low, x):
        return jnp.concatenate([dot(top, x[:HALF], 1, 0), dot(low, x, 1, 0)], axis=0)

    def down(top, low, x):
        both = dot(low, x[HALF:], 0, 0)
        return jnp.concatenate([dot(top, x[:HALF], 0, 0) + both[:HALF], both[HALF:]], axis=0)

    for n in range(blocks):
        r = slice(n * SPAN, (n + 1) * SPAN)
        q, k, v, g = q_ref[r, cols], k_ref[r, cols], v_ref[r, cols], g_ref[r, cols]
        s0, s1 = lower(q, k)
        d0, d1 = lower(g, v)
        o_ref[r, cols] = across(s0, s1, v)
        gq_ref[r, cols] = across(d0, d1, k)
        gk_ref[r, cols] = down(d0, d1, q)
        gv_ref[r, cols] = down(s0, s1, g)


def local_products(scale, h, xs, parts):
    rows, width = xs[0].shape
    blocks = rows // SPAN
    return pl.pallas_call(
        functools.partial(local_kernel, scale, h, blocks),
        in_specs=[VM] * (4 + len(parts)),
        out_specs=[VM] * 4,
        out_shape=[pltpu.VMEM((rows, width), F32)] * 4,
        input_output_aliases={4 + i: i for i in range(len(parts))},
        compiler_params=pltpu.CompilerParams(vmem_limit_bytes=16 * 2**20),
        cost_estimate=pl.CostEstimate(flops=LOCAL_FLOPS, bytes_accessed=1024, transcendentals=0),
        name="local_products",
    )(*xs, *parts)


def ready_kernel(g0, g1, g2, g3, pair, *outs):
    y, z, way = lax.axis_index("seq") & 3, lax.axis_index("seq") >> 2, side()
    got = [(r[:DH], r[DH:]) for r in (g0, g1, g2, g3)]

    def when(c, x):
        return jnp.where(c, x, 0.0)

    kv = when((z & 1) != 0, pair[:DH])
    qg = when((z & 1) == 0, pair[DH:])
    for e, out in enumerate(outs):
        dst = (y + way * e) & 3
        a, b = kv, qg
        for d in range(NY):
            src = (y - way * d) & 3
            a = a + when(src < dst, got[d][0])
            b = b + when(src > dst, got[d][1])
        out[:DH] = a
        out[DH:] = b


def make_ready(*arrays):
    return pl.pallas_call(
        ready_kernel,
        in_specs=[VM] * len(arrays),
        out_specs=[VM] * NY,
        out_shape=[jax.ShapeDtypeStruct((2 * DH, DH), F32)] * NY,
        compiler_params=pltpu.CompilerParams(vmem_limit_bytes=8 * 2**20),
        name="make_ready",
    )(*arrays)


def carry_kernel(scale, steps, blocks, *refs):
    xs, parts, cums, refs = refs[:4], refs[4:8], refs[8:10], refs[10:]
    priors, outs, stage, sems = refs[: len(steps)], refs[-6:-2], refs[-2], refs[-1]
    q, k, v, g = xs
    copies = []
    for i, (d, prior) in enumerate(zip(steps, priors)):
        h = (lax.axis_index("seq") - side() * d) & 3
        cols = pl.ds(pl.multiple_of(h * DH, DH), DH)
        cum = cums[1].at[HEADS - 1 - d] if d else cums[0].at[0]
        for n in range(blocks):
            kv, qg = prior[:DH], prior[DH:]
            if n > 0:
                kv = kv + cum[n - 1, :DH]
            if n < blocks - 1:
                qg = qg + cum[n, DH:]
            kv, qg = kv * scale, qg * scale
            todo = ((q, stacked(kv, 0), 0), (g, stacked(kv, 1), 1), (v, stacked(qg, 1), 1), (k, stacked(qg, 0), 0))
            end = n == blocks - 1 and i == len(steps) - 1
            for m, part in enumerate((HALF, HALF) if end else (SPAN,)):
                r = pl.ds(n * SPAN + m * HALF, part)
                for j, (x, w, c) in enumerate(todo):
                    add = dot(twice(x[r, cols]), w, 1, c)
                    stage[i, j, r] = (parts[j][r, cols] + add).astype(BF16)
                    copy = pltpu.make_async_copy(stage.at[i, j, r], outs[j].at[r, cols], sems.at[i, j, n + m])
                    copy.start()
                    copies.append(copy)
    for copy in copies:
        copy.wait()


def add_carry(scale, steps, xs, parts, cums, priors, before):
    rows, width = xs[0].shape
    blocks = rows // SPAN
    m = len(steps)
    return pl.pallas_call(
        functools.partial(carry_kernel, scale, steps, blocks),
        in_specs=[VM] * (10 + m) + [HB] * len(before),
        out_specs=[HB] * 4,
        out_shape=[pltpu.HBM((rows, width), BF16)] * 4,
        input_output_aliases={10 + m + i: i for i in range(len(before))},
        scratch_shapes=[pltpu.VMEM((m, 4, rows, DH), BF16), pltpu.SemaphoreType.DMA((m, 4, blocks + 1))],
        compiler_params=pltpu.CompilerParams(vmem_limit_bytes=16 * 2**20),
        cost_estimate=pl.CostEstimate(flops=m * 1_500_000_000, bytes_accessed=1024, transcendentals=0),
        name="add_carry",
    )(*xs, *parts, *cums, *priors, *before)


def moves(zmap, ymap):
    return [(z * NY + y, zmap(z) * NY + ymap(y)) for z in range(NZ) for y in range(NY)]


def on_device(query, key_in, value, grad_out):
    rows = query.shape[0]
    scale = 1.0 / math.sqrt(DH * rows * lax.axis_size("seq"))
    blocks = rows // SPAN
    inputs = [pltpu.with_memory_space_constraint(x, pltpu.HBM) for x in (query, key_in, value, grad_out)]

    def swap(x, zmap):
        return lax.ppermute(x, "seq", moves(zmap, lambda b: b))

    def turn(x, d):
        ring = NY * NZ
        pairs = [
            (p * ring + i, p * ring + j)
            for p in range(lax.axis_size("dp"))
            for i, j in moves(lambda a: a, lambda b: (b + (1 - 2 * (p & 1)) * d) % NY)
        ]
        return lax.ppermute(x, ("dp", "seq"), pairs)

    q, k, v, g, *own, others, high, up = device_sums(*inputs)
    xs = (q, k, v, g)
    high, up = high > 0.5, up > 0.5
    sent = [turn(own[d - 1], d) for d in range(1, NY)]
    mine, inner = own_sums(xs)
    got = [mine] + sent
    parts = ()
    for h in range(HEADS):
        parts = local_products(scale, h, xs, parts)
    total = got[0] + got[1] + got[2] + got[3]
    pair = swap(total, lambda a: a ^ 1)
    total = total + pair
    four = swap(jnp.where(up, total[DH:], total[:DH]), lambda a: a ^ 3)
    across = jnp.where(high, total[DH:], total[:DH])
    eight = swap(across, lambda a: a ^ 5), swap(across, lambda a: 7 - a)
    eight = eight[0] + eight[1]
    last = jnp.concatenate(
        [
            jnp.where(up, four, 0.0) + jnp.where(high, eight, 0.0),
            jnp.where(up, 0.0, four) + jnp.where(high, 0.0, eight),
        ],
        axis=0,
    )
    ready = [x + last for x in make_ready(*got, pair)]
    prior = {0: ready[0]} | {d: turn(ready[d], d) for d in (2, 3, 1)}
    outs = ()
    for steps in ((0,), (1, 2, 3)):
        outs = add_carry(scale, steps, xs, parts, (inner, others), [prior[d] for d in steps], outs)
    return tuple(outs)


def solution(mesh):
    spec = P("seq", "dp")
    return jax.shard_map(
        on_device,
        mesh=mesh,
        in_specs=(spec,) * 4,
        out_specs=(spec,) * 4,
        check_vma=False,
    )
```

```python
import functools
import math

import jax
import jax.numpy as jnp
from jax import lax
from jax.experimental import pallas as pl
from jax.experimental.pallas import tpu as pltpu
from jax.sharding import PartitionSpec as P

DH = 128
SPAN = 512
HALF = SPAN // 2
HEADS = 4
NY = 4
NZ = 8
LOCAL_FLOPS = 2_000_000_000
F32 = jnp.float32
BF16 = jnp.bfloat16
VM = pl.BlockSpec(memory_space=pltpu.VMEM)
SM = pl.BlockSpec(memory_space=pltpu.SMEM)
HB = pl.BlockSpec(memory_space=pltpu.HBM)


def dot(a, b, ca, cb):
    return lax.dot_general(a, b, (((ca,), (cb,)), ((), ())), preferred_element_type=F32)


def twice(x):
    return jnp.concatenate([x, x], axis=1)


def stacked(s, axis):
    hi = s.astype(BF16)
    lo = (s - hi.astype(F32)).astype(BF16)
    return jnp.concatenate([hi, lo], axis=axis)


def at(n, h):
    return slice(n * SPAN, (n + 1) * SPAN), slice(h * DH, (h + 1) * DH)


CHUNKS = ((0, 512), (512, 512), (1024, 256), (1280, 256))


def head_sums(me_ref, xs, d, out, cum):
    q, k, v, g = xs
    cols = pl.ds(pl.multiple_of(((me_ref[0] + d) & 3) * DH, DH), DH)
    state = {"kv": 0.0, "first": 0.0}

    def step(n):
        start, size = CHUNKS[n]
        block, r = start // SPAN, slice(start, start + size)
        qg = dot(q[r, cols], g[r, cols], 0, 0)
        state["kv"] = state["kv"] + dot(k[r, cols], v[r, cols], 0, 0)
        for j in range(min(block, cum.shape[0])):
            if block == j + 1 and start % SPAN == 0:
                cum[j, DH:] = qg
            else:
                cum[j, DH:] += qg
        if block == 0:
            state["first"] = state["first"] + qg
        if (start + size) % SPAN == 0 and block < cum.shape[0]:
            cum[block, :DH] = state["kv"]

    def finish():
        out[:DH] = state["kv"]
        out[DH:] = state["first"] + cum[0, DH:]

    return step, finish


def sums_kernel(me_ref, high_ref, up_ref, *refs):
    srcs, dsts, outs, cum, sems = refs[:4], refs[4:8], refs[8:11], refs[11], refs[12]
    copies = []
    for n, (start, size) in enumerate(CHUNKS):
        rows = pl.ds(start, size)
        copies.append([pltpu.make_async_copy(srcs[i].at[rows], dsts[i].at[rows], sems.at[n, i]) for i in range(4)])
    for row in copies:
        for c in row:
            c.start()
    heads = [head_sums(me_ref, dsts, d + 1, outs[d], cum.at[d]) for d in range(3)]
    for n in range(len(CHUNKS)):
        for c in copies[n]:
            c.wait()
        for step, _ in heads:
            step(n)
    for _, finish in heads:
        finish()


def device_sums(me, high, up, q, k, v, g):
    rows, width = q.shape
    one = jax.ShapeDtypeStruct((2 * DH, DH), F32)
    return pl.pallas_call(
        sums_kernel,
        in_specs=[SM] * 3 + [HB] * 4,
        out_specs=[VM] * 8,
        out_shape=[pltpu.VMEM((rows, width), BF16)] * 4 + [one] * 3 + [pltpu.VMEM((3, rows // SPAN - 1, 2 * DH, DH), F32)],
        scratch_shapes=[pltpu.SemaphoreType.DMA((len(CHUNKS), 4))],
        compiler_params=pltpu.CompilerParams(vmem_limit_bytes=16 * 2**20),
        name="device_sums",
    )(me, high, up, q, k, v, g)


def own_kernel(me_ref, q, k, v, g, out, cum):
    step, finish = head_sums(me_ref, (q, k, v, g), 0, out, cum.at[0])
    for n in range(len(CHUNKS)):
        step(n)
    finish()


def own_sums(me, xs):
    rows = xs[0].shape[0]
    return pl.pallas_call(
        own_kernel,
        in_specs=[SM] + [VM] * 4,
        out_specs=[VM] * 2,
        out_shape=[jax.ShapeDtypeStruct((2 * DH, DH), F32), pltpu.VMEM((1, rows // SPAN - 1, 2 * DH, DH), F32)],
        compiler_params=pltpu.CompilerParams(vmem_limit_bytes=8 * 2**20),
        cost_estimate=pl.CostEstimate(flops=100_000_000, bytes_accessed=1024, transcendentals=0),
        name="own_sums",
    )(me, *xs)


def local_kernel(scale, h, blocks, q_ref, k_ref, v_ref, g_ref, *refs):
    o_ref, gq_ref, gk_ref, gv_ref = refs[-4:]
    cols = slice(h * DH, (h + 1) * DH)
    t = lax.broadcasted_iota(jnp.int32, (HALF, HALF), 0)
    s = lax.broadcasted_iota(jnp.int32, (HALF, HALF), 1)
    keep = t >= s

    def lower(a, b):
        top = jnp.where(keep, scale * dot(a[:HALF], b[:HALF], 1, 1), 0.0).astype(BF16)
        low = scale * dot(a[HALF:], b, 1, 1)
        right = jnp.where(keep, low[:, HALF:], 0.0)
        return top, jnp.concatenate([low[:, :HALF].astype(BF16), right.astype(BF16)], axis=1)

    def across(top, low, x):
        return jnp.concatenate([dot(top, x[:HALF], 1, 0), dot(low, x, 1, 0)], axis=0)

    def down(top, low, x):
        both = dot(low, x[HALF:], 0, 0)
        return jnp.concatenate([dot(top, x[:HALF], 0, 0) + both[:HALF], both[HALF:]], axis=0)

    for n in range(blocks):
        r = slice(n * SPAN, (n + 1) * SPAN)
        q, k, v, g = q_ref[r, cols], k_ref[r, cols], v_ref[r, cols], g_ref[r, cols]
        s0, s1 = lower(q, k)
        d0, d1 = lower(g, v)
        o_ref[r, cols] = across(s0, s1, v)
        gq_ref[r, cols] = across(d0, d1, k)
        gk_ref[r, cols] = down(d0, d1, q)
        gv_ref[r, cols] = down(s0, s1, g)


def local_products(scale, h, xs, parts):
    rows, width = xs[0].shape
    blocks = rows // SPAN
    return pl.pallas_call(
        functools.partial(local_kernel, scale, h, blocks),
        in_specs=[VM] * (4 + len(parts)),
        out_specs=[VM] * 4,
        out_shape=[pltpu.VMEM((rows, width), F32)] * 4,
        input_output_aliases={4 + i: i for i in range(len(parts))},
        compiler_params=pltpu.CompilerParams(vmem_limit_bytes=16 * 2**20),
        cost_estimate=pl.CostEstimate(flops=LOCAL_FLOPS, bytes_accessed=1024, transcendentals=0),
        name="local_products",
    )(*xs, *parts)


def ready_kernel(me_ref, g0, g1, g2, g3, pair, *outs):
    y, z = me_ref[0] & 3, me_ref[0] >> 2
    got = [(r[:DH], r[DH:]) for r in (g0, g1, g2, g3)]

    def when(c, x):
        return jnp.where(c, x, 0.0)

    kv = when((z & 1) != 0, pair[:DH])
    qg = when((z & 1) == 0, pair[DH:])
    for e, out in enumerate(outs):
        dst = (y + e) & 3
        a, b = kv, qg
        for d in range(NY):
            src = (y - d) & 3
            a = a + when(src < dst, got[d][0])
            b = b + when(src > dst, got[d][1])
        out[:DH] = a
        out[DH:] = b


def make_ready(me, *arrays):
    return pl.pallas_call(
        ready_kernel,
        in_specs=[SM] + [VM] * len(arrays),
        out_specs=[VM] * NY,
        out_shape=[jax.ShapeDtypeStruct((2 * DH, DH), F32)] * NY,
        compiler_params=pltpu.CompilerParams(vmem_limit_bytes=8 * 2**20),
        name="make_ready",
    )(me, *arrays)


def carry_kernel(scale, steps, blocks, me_ref, *refs):
    xs, parts, cums, refs = refs[:4], refs[4:8], refs[8:10], refs[10:]
    priors, outs, stage, sems = refs[: len(steps)], refs[-6:-2], refs[-2], refs[-1]
    q, k, v, g = xs
    copies = []
    for i, (d, prior) in enumerate(zip(steps, priors)):
        h = (me_ref[0] - d) & 3
        cols = pl.ds(pl.multiple_of(h * DH, DH), DH)
        cum = cums[1].at[HEADS - 1 - d] if d else cums[0].at[0]
        for n in range(blocks):
            kv, qg = prior[:DH], prior[DH:]
            if n > 0:
                kv = kv + cum[n - 1, :DH]
            if n < blocks - 1:
                qg = qg + cum[n, DH:]
            kv, qg = kv * scale, qg * scale
            todo = ((q, stacked(kv, 0), 0), (g, stacked(kv, 1), 1), (v, stacked(qg, 1), 1), (k, stacked(qg, 0), 0))
            end = n == blocks - 1 and i == len(steps) - 1
            for m, part in enumerate((HALF, HALF) if end else (SPAN,)):
                r = pl.ds(n * SPAN + m * HALF, part)
                for j, (x, w, c) in enumerate(todo):
                    add = dot(twice(x[r, cols]), w, 1, c)
                    stage[i, j, r] = (parts[j][r, cols] + add).astype(BF16)
                    copy = pltpu.make_async_copy(stage.at[i, j, r], outs[j].at[r, cols], sems.at[i, j, n + m])
                    copy.start()
                    copies.append(copy)
    for copy in copies:
        copy.wait()


def add_carry(scale, me, steps, xs, parts, cums, priors, before):
    rows, width = xs[0].shape
    blocks = rows // SPAN
    m = len(steps)
    return pl.pallas_call(
        functools.partial(carry_kernel, scale, steps, blocks),
        in_specs=[SM] + [VM] * (10 + m) + [HB] * len(before),
        out_specs=[HB] * 4,
        out_shape=[pltpu.HBM((rows, width), BF16)] * 4,
        input_output_aliases={11 + m + i: i for i in range(len(before))},
        scratch_shapes=[pltpu.VMEM((m, 4, rows, DH), BF16), pltpu.SemaphoreType.DMA((m, 4, blocks + 1))],
        compiler_params=pltpu.CompilerParams(vmem_limit_bytes=16 * 2**20),
        cost_estimate=pl.CostEstimate(flops=m * 1_500_000_000, bytes_accessed=1024, transcendentals=0),
        name="add_carry",
    )(me, *xs, *parts, *cums, *priors, *before)


def moves(zmap, ymap):
    return [(z * NY + y, zmap(z) * NY + ymap(y)) for z in range(NZ) for y in range(NY)]


def on_device(query, key_in, value, grad_out):
    rows = query.shape[0]
    scale = 1.0 / math.sqrt(DH * rows * lax.axis_size("seq"))
    blocks = rows // SPAN
    index = lax.axis_index("seq")
    me = index.reshape(1)
    inputs = [pltpu.with_memory_space_constraint(x, pltpu.HBM) for x in (query, key_in, value, grad_out)]

    def swap(x, zmap):
        return lax.ppermute(x, "seq", moves(zmap, lambda b: b))

    def split_swap(x, even, odd):
        ring = NY * NZ
        pairs = [
            (p * ring + i, p * ring + j)
            for p in range(lax.axis_size("dp"))
            for i, j in moves(lambda a: a ^ (odd if p & 1 else even), lambda b: b)
        ]
        return lax.ppermute(x, ("dp", "seq"), pairs)

    def turn(x, d):
        return lax.ppermute(x, "seq", moves(lambda a: a, lambda b: (b + d) % NY))

    high, up = index >= NY * NZ // 2, (index & (2 * NY)) != 0
    flags = [c.astype(jnp.int32).reshape(1) for c in (high, up)]
    q, k, v, g, *own, others = device_sums(me, *flags, *inputs)
    xs = (q, k, v, g)
    sent = [turn(own[d - 1], d) for d in range(1, NY)]
    mine, inner = own_sums(me, xs)
    got = [mine] + sent
    parts = ()
    for h in range(HEADS):
        parts = local_products(scale, h, xs, parts)
    total = got[0] + got[1] + got[2] + got[3]
    pair = swap(total, lambda a: a ^ 1)
    total = total + pair
    four = swap(jnp.where(up, total[DH:], total[:DH]), lambda a: a ^ 3)
    across = jnp.where(high, total[DH:], total[:DH])
    eight = split_swap(across, 5, 7), split_swap(across, 7, 5)
    eight = eight[0] + eight[1]
    last = jnp.concatenate(
        [
            jnp.where(up, four, 0.0) + jnp.where(high, eight, 0.0),
            jnp.where(up, 0.0, four) + jnp.where(high, 0.0, eight),
        ],
        axis=0,
    )
    ready = [x + last for x in make_ready(me, *got, pair)]
    prior = {0: ready[0]} | {d: turn(ready[d], d) for d in (2, 3, 1)}
    outs = ()
    for steps in ((0,), (1, 2, 3)):
        outs = add_carry(scale, me, steps, xs, parts, (inner, others), [prior[d] for d in steps], outs)
    return tuple(outs)


def solution(mesh):
    spec = P("seq", "dp")
    return jax.shard_map(
        on_device,
        mesh=mesh,
        in_specs=(spec,) * 4,
        out_specs=(spec,) * 4,
        check_vma=False,
    )
```

```python
import functools
import math

import jax
import jax.numpy as jnp
from jax import lax
from jax.experimental import pallas as pl
from jax.experimental.pallas import tpu as pltpu
from jax.sharding import PartitionSpec as P

DH = 128
SPAN = 512
HALF = SPAN // 2
HEADS = 4
NY = 4
NZ = 8
LOCAL_FLOPS = 2_000_000_000
F32 = jnp.float32
BF16 = jnp.bfloat16
VM = pl.BlockSpec(memory_space=pltpu.VMEM)
SM = pl.BlockSpec(memory_space=pltpu.SMEM)
HB = pl.BlockSpec(memory_space=pltpu.HBM)


def dot(a, b, ca, cb):
    return lax.dot_general(a, b, (((ca,), (cb,)), ((), ())), preferred_element_type=F32)


def twice(x):
    return jnp.concatenate([x, x], axis=1)


def stacked(s, axis):
    hi = s.astype(BF16)
    lo = (s - hi.astype(F32)).astype(BF16)
    return jnp.concatenate([hi, lo], axis=axis)


def at(n, h):
    return slice(n * SPAN, (n + 1) * SPAN), slice(h * DH, (h + 1) * DH)


CHUNKS = ((0, 512), (512, 512), (1024, 256), (1280, 256))


def head_sums(me_ref, xs, d, out, cum):
    q, k, v, g = xs
    cols = pl.ds(pl.multiple_of(((me_ref[0] + d) & 3) * DH, DH), DH)
    state = {"kv": 0.0, "first": 0.0}

    def step(n):
        start, size = CHUNKS[n]
        block, r = start // SPAN, slice(start, start + size)
        qg = dot(q[r, cols], g[r, cols], 0, 0)
        state["kv"] = state["kv"] + dot(k[r, cols], v[r, cols], 0, 0)
        for j in range(min(block, cum.shape[0])):
            if block == j + 1 and start % SPAN == 0:
                cum[j, DH:] = qg
            else:
                cum[j, DH:] += qg
        if block == 0:
            state["first"] = state["first"] + qg
        if (start + size) % SPAN == 0 and block < cum.shape[0]:
            cum[block, :DH] = state["kv"]

    def finish():
        out[:DH] = state["kv"]
        out[DH:] = state["first"] + cum[0, DH:]

    return step, finish


def sums_kernel(me_ref, high_ref, up_ref, *refs):
    srcs, dsts, outs, cum, sems = refs[:4], refs[4:8], refs[8:11], refs[11], refs[12]
    copies = []
    for n, (start, size) in enumerate(CHUNKS):
        rows = pl.ds(start, size)
        copies.append([pltpu.make_async_copy(srcs[i].at[rows], dsts[i].at[rows], sems.at[n, i]) for i in range(4)])
    for row in copies:
        for c in row:
            c.start()
    heads = [head_sums(me_ref, dsts, d + 1, outs[d], cum.at[d]) for d in range(3)]
    for n in range(len(CHUNKS)):
        for c in copies[n]:
            c.wait()
        for step, _ in heads:
            step(n)
    for _, finish in heads:
        finish()


def device_sums(me, high, up, q, k, v, g):
    rows, width = q.shape
    one = jax.ShapeDtypeStruct((2 * DH, DH), F32)
    return pl.pallas_call(
        sums_kernel,
        in_specs=[SM] * 3 + [HB] * 4,
        out_specs=[VM] * 8,
        out_shape=[pltpu.VMEM((rows, width), BF16)] * 4 + [one] * 3 + [pltpu.VMEM((3, rows // SPAN - 1, 2 * DH, DH), F32)],
        scratch_shapes=[pltpu.SemaphoreType.DMA((len(CHUNKS), 4))],
        compiler_params=pltpu.CompilerParams(vmem_limit_bytes=16 * 2**20),
        name="device_sums",
    )(me, high, up, q, k, v, g)


def own_kernel(me_ref, q, k, v, g, out, cum):
    step, finish = head_sums(me_ref, (q, k, v, g), 0, out, cum.at[0])
    for n in range(len(CHUNKS)):
        step(n)
    finish()


def own_sums(me, xs):
    rows = xs[0].shape[0]
    return pl.pallas_call(
        own_kernel,
        in_specs=[SM] + [VM] * 4,
        out_specs=[VM] * 2,
        out_shape=[jax.ShapeDtypeStruct((2 * DH, DH), F32), pltpu.VMEM((1, rows // SPAN - 1, 2 * DH, DH), F32)],
        compiler_params=pltpu.CompilerParams(vmem_limit_bytes=8 * 2**20),
        cost_estimate=pl.CostEstimate(flops=100_000_000, bytes_accessed=1024, transcendentals=0),
        name="own_sums",
    )(me, *xs)


def local_kernel(scale, h, blocks, q_ref, k_ref, v_ref, g_ref, *refs):
    o_ref, gq_ref, gk_ref, gv_ref = refs[-4:]
    cols = slice(h * DH, (h + 1) * DH)
    t = lax.broadcasted_iota(jnp.int32, (HALF, HALF), 0)
    s = lax.broadcasted_iota(jnp.int32, (HALF, HALF), 1)
    keep = t >= s

    def lower(a, b):
        top = jnp.where(keep, scale * dot(a[:HALF], b[:HALF], 1, 1), 0.0).astype(BF16)
        low = scale * dot(a[HALF:], b, 1, 1)
        right = jnp.where(keep, low[:, HALF:], 0.0)
        return top, jnp.concatenate([low[:, :HALF].astype(BF16), right.astype(BF16)], axis=1)

    def across(top, low, x):
        return jnp.concatenate([dot(top, x[:HALF], 1, 0), dot(low, x, 1, 0)], axis=0)

    def down(top, low, x):
        both = dot(low, x[HALF:], 0, 0)
        return jnp.concatenate([dot(top, x[:HALF], 0, 0) + both[:HALF], both[HALF:]], axis=0)

    for n in range(blocks):
        r = slice(n * SPAN, (n + 1) * SPAN)
        q, k, v, g = q_ref[r, cols], k_ref[r, cols], v_ref[r, cols], g_ref[r, cols]
        s0, s1 = lower(q, k)
        d0, d1 = lower(g, v)
        o_ref[r, cols] = across(s0, s1, v)
        gq_ref[r, cols] = across(d0, d1, k)
        gk_ref[r, cols] = down(d0, d1, q)
        gv_ref[r, cols] = down(s0, s1, g)


def local_products(scale, h, xs, parts):
    rows, width = xs[0].shape
    blocks = rows // SPAN
    return pl.pallas_call(
        functools.partial(local_kernel, scale, h, blocks),
        in_specs=[VM] * (4 + len(parts)),
        out_specs=[VM] * 4,
        out_shape=[pltpu.VMEM((rows, width), F32)] * 4,
        input_output_aliases={4 + i: i for i in range(len(parts))},
        compiler_params=pltpu.CompilerParams(vmem_limit_bytes=16 * 2**20),
        cost_estimate=pl.CostEstimate(flops=LOCAL_FLOPS, bytes_accessed=1024, transcendentals=0),
        name="local_products",
    )(*xs, *parts)


def ready_kernel(me_ref, g0, g1, g2, g3, pair, *outs):
    y, z = me_ref[0] & 3, me_ref[0] >> 2
    got = [(r[:DH], r[DH:]) for r in (g0, g1, g2, g3)]

    def when(c, x):
        return jnp.where(c, x, 0.0)

    kv = when((z & 1) != 0, pair[:DH])
    qg = when((z & 1) == 0, pair[DH:])
    for e, out in enumerate(outs):
        dst = (y + e) & 3
        a, b = kv, qg
        for d in range(NY):
            src = (y - d) & 3
            a = a + when(src < dst, got[d][0])
            b = b + when(src > dst, got[d][1])
        out[:DH] = a
        out[DH:] = b


def make_ready(me, *arrays):
    return pl.pallas_call(
        ready_kernel,
        in_specs=[SM] + [VM] * len(arrays),
        out_specs=[VM] * NY,
        out_shape=[jax.ShapeDtypeStruct((2 * DH, DH), F32)] * NY,
        compiler_params=pltpu.CompilerParams(vmem_limit_bytes=8 * 2**20),
        name="make_ready",
    )(me, *arrays)


def carry_kernel(scale, steps, blocks, me_ref, *refs):
    xs, parts, cums, refs = refs[:4], refs[4:8], refs[8:10], refs[10:]
    priors, outs, stage, sems = refs[: len(steps)], refs[-6:-2], refs[-2], refs[-1]
    q, k, v, g = xs
    copies = []
    for i, (d, prior) in enumerate(zip(steps, priors)):
        h = (me_ref[0] - d) & 3
        cols = pl.ds(pl.multiple_of(h * DH, DH), DH)
        cum = cums[1].at[HEADS - 1 - d] if d else cums[0].at[0]
        for n in range(blocks):
            kv, qg = prior[:DH], prior[DH:]
            if n > 0:
                kv = kv + cum[n - 1, :DH]
            if n < blocks - 1:
                qg = qg + cum[n, DH:]
            kv, qg = kv * scale, qg * scale
            todo = ((q, stacked(kv, 0), 0), (g, stacked(kv, 1), 1), (v, stacked(qg, 1), 1), (k, stacked(qg, 0), 0))
            end = n == blocks - 1 and i == len(steps) - 1
            for m, part in enumerate((HALF, HALF) if end else (SPAN,)):
                r = pl.ds(n * SPAN + m * HALF, part)
                for j, (x, w, c) in enumerate(todo):
                    add = dot(twice(x[r, cols]), w, 1, c)
                    stage[i, j, r] = (parts[j][r, cols] + add).astype(BF16)
                    copy = pltpu.make_async_copy(stage.at[i, j, r], outs[j].at[r, cols], sems.at[i, j, n + m])
                    copy.start()
                    copies.append(copy)
    for copy in copies:
        copy.wait()


def add_carry(scale, me, steps, xs, parts, cums, priors, before):
    rows, width = xs[0].shape
    blocks = rows // SPAN
    m = len(steps)
    return pl.pallas_call(
        functools.partial(carry_kernel, scale, steps, blocks),
        in_specs=[SM] + [VM] * (10 + m) + [HB] * len(before),
        out_specs=[HB] * 4,
        out_shape=[pltpu.HBM((rows, width), BF16)] * 4,
        input_output_aliases={11 + m + i: i for i in range(len(before))},
        scratch_shapes=[pltpu.VMEM((m, 4, rows, DH), BF16), pltpu.SemaphoreType.DMA((m, 4, blocks + 1))],
        compiler_params=pltpu.CompilerParams(vmem_limit_bytes=16 * 2**20),
        cost_estimate=pl.CostEstimate(flops=m * 1_500_000_000, bytes_accessed=1024, transcendentals=0),
        name="add_carry",
    )(me, *xs, *parts, *cums, *priors, *before)


def moves(zmap, ymap):
    return [(z * NY + y, zmap(z) * NY + ymap(y)) for z in range(NZ) for y in range(NY)]


def on_device(query, key_in, value, grad_out):
    rows = query.shape[0]
    scale = 1.0 / math.sqrt(DH * rows * lax.axis_size("seq"))
    blocks = rows // SPAN
    index = lax.axis_index("seq")
    me = index.reshape(1)
    inputs = [pltpu.with_memory_space_constraint(x, pltpu.HBM) for x in (query, key_in, value, grad_out)]

    def swap(x, zmap):
        return lax.ppermute(x, "seq", moves(zmap, lambda b: b))

    def turn(x, d):
        return lax.ppermute(x, "seq", moves(lambda a: a, lambda b: (b + d) % NY))

    high, up = index >= NY * NZ // 2, (index & (2 * NY)) != 0
    flags = [c.astype(jnp.int32).reshape(1) for c in (high, up)]
    q, k, v, g, *own, others = device_sums(me, *flags, *inputs)
    xs = (q, k, v, g)
    sent = [turn(own[d - 1], d) for d in range(1, NY)]
    mine, inner = own_sums(me, xs)
    got = [mine] + sent
    parts = ()
    for h in range(HEADS):
        parts = local_products(scale, h, xs, parts)
    total = got[0] + got[1] + got[2] + got[3]
    pair = swap(total, lambda a: a ^ 1)
    total = total + pair
    four = swap(jnp.where(up, total[DH:], total[:DH]), lambda a: a ^ 2)
    across = jnp.where(high, total[DH:], total[:DH])
    eight = swap(across, lambda a: a ^ 5), swap(across, lambda a: 7 - a)
    eight = eight[0] + eight[1]
    last = jnp.concatenate(
        [
            jnp.where(up, four, 0.0) + jnp.where(high, eight, 0.0),
            jnp.where(up, 0.0, four) + jnp.where(high, 0.0, eight),
        ],
        axis=0,
    )
    ready = [x + last for x in make_ready(me, *got, pair)]
    prior = {0: ready[0]} | {d: turn(ready[d], d) for d in (2, 3, 1)}
    outs = ()
    for steps in ((0,), (1, 2, 3)):
        outs = add_carry(scale, me, steps, xs, parts, (inner, others), [prior[d] for d in steps], outs)
    return tuple(outs)


def solution(mesh):
    spec = P("seq", "dp")
    return jax.shard_map(
        on_device,
        mesh=mesh,
        in_specs=(spec,) * 4,
        out_specs=(spec,) * 4,
        check_vma=False,
    )
```
